32 devices in a mesh: runs: 2 (over x), patch: 8 (over z, y), sub: 2 (over core).
Axes of the slice: x: 2, y: 2, z: 4, core: 2. Of those that a mesh axis runs over, the one named last changes fastest.
Arguments:
- eta_c: float32 [6144, 768], P(('runs', 'patch', 'sub')), parts along dimension 0, may hold values from -4 to 4
- u_c: float32 [6144, 768], P(('runs', 'patch', 'sub')), parts along dimension 0, may hold values from -4 to 4
- v_c: float32 [6144, 768], P(('runs', 'patch', 'sub')), parts along dimension 0, may hold values from -4 to 4
- depth_c: float32 [6144, 768], P(('runs', 'patch', 'sub')), parts along dimension 0, may hold values from 0.2 to 1
- eta_f: float32 [12288, 512], P(('runs', 'patch', 'sub')), parts along dimension 0, may hold values from -4 to 4
- u_f: float32 [12288, 512], P(('runs', 'patch', 'sub')), parts along dimension 0, may hold values from -4 to 4
- v_f: float32 [12288, 512], P(('runs', 'patch', 'sub')), parts along dimension 0, may hold values from -4 to 4
- wet_f: int32 [12288, 512], P(('runs', 'patch', 'sub')), parts along dimension 0, may hold values 0 or 1
- topography: float32 [3072, 2, 512], P(('runs', 'patch', 'sub')), parts along dimension 0, may hold values from 0.2 to 1
- owner_list: int32 [6144, 1], P('runs'), parts along dimension 0, may hold values from 0 to 7; in each aligned block of 192 rows (0 to 191, 192 to 383, ...) at most 48 rows name the same one
- block_list: int32 [6144], P('runs'), parts along dimension 0, may hold values from 0 to 95
- fault_row: float32 [512], P(('runs', 'patch', 'sub')), parts along dimension 0, may hold values from 0 to 3072
- fault_col: float32 [512], P(('runs', 'patch', 'sub')), parts along dimension 0, may hold values from 0 to 768
- fault_width: float32 [512], P(('runs', 'patch', 'sub')), parts along dimension 0, may hold values from 3 to 12
- fault_slip: float32 [512], P(('runs', 'patch', 'sub')), parts along dimension 0, may hold values from -5 to 5
Outputs:
- eta_c_out: float32 [6144, 768], P(('runs', 'patch', 'sub')), parts along dimension 0
- u_c_out: float32 [6144, 768], P(('runs', 'patch', 'sub')), parts along dimension 0
- v_c_out: float32 [6144, 768], P(('runs', 'patch', 'sub')), parts along dimension 0
- eta_f_out: float32 [12288, 512], P(('runs', 'patch', 'sub')), parts along dimension 0
- u_f_out: float32 [12288, 512], P(('runs', 'patch', 'sub')), parts along dimension 0
- v_f_out: float32 [12288, 512], P(('runs', 'patch', 'sub')), parts along dimension 0
The draws below stay inside these ranges and needn't reach their ends.
There are 2 independent parts, one for each index of `runs`. The reference program is written for one: setup_inputs(seed, part) draws one part's arguments, and reference() takes and returns one part's arrays. A program takes and returns all parts, laid end to end along the dimension named above; each array names one. Nothing has to cross between parts.
Inputs may be any that keep to these rules, and one draw needn't show every extreme that they name: `owner_list`: within each device's 192 fine blocks no owner is named more than 48 times, a bound that some block reaches.
All inputs are finite; a program needn't handle non-finite values. No bound on the sum of `wet_f` on one device may be relied on, other than what follows from the above.
Results may differ from the reference program's by a relative error of at most 0.0003.
Values sent between devices are 32-bit elements; how exact they have to be, the bound alone decides.
A program may use at most 64 MiB of HBM per device.

```python
import math
import jax
import jax.numpy as jnp
import numpy as np
from jax import lax

CY = 192
CX = 768
FX = 512
FP = 2
DEV = 16
NYC = 3072
NYF = 6144
NP = 192
TB = 96
CAP = 48
NF = 256
N_PATCH = 8
N_SUB = 2


def plant(entries, own_key, least, high):
    place = [jax.random.randint(jax.random.fold_in(own_key, axis), (), 0, length) for axis, length in enumerate(entries.shape)]
    widest = entries.shape.index(max(entries.shape))
    beside = place[:widest] + [(place[widest] + 1) % entries.shape[widest]] + place[widest + 1:]
    return entries.at[tuple(place)].set(least).at[tuple(beside)].set(high)


def shard_levels(stream_key, extent, cuts, smallest, high):
    factor_of = 1.0
    for position, parts in cuts:
        heights = jax.random.uniform(jax.random.fold_in(jax.random.fold_in(stream_key, 6), position), (parts,), jnp.float32, smallest / len(cuts), high / len(cuts))
        factor_of = factor_of * jnp.repeat(jnp.exp(heights), extent[position] // parts).reshape((-1,) + (1,) * (len(extent) - 1 - position))
    return factor_of


def shared_out(stream_key, own, number, rows, number_of, top, limit, slope):
    order = jax.random.permutation(stream_key, number_of)
    crowded, common = portions_of(number_of, rows * top, limit, slope, True), portions_of(number_of, rows * top, limit, slope, False)
    places = jnp.arange(number_of)

    def named(lengths, turn):
        used = int((lengths > 0).sum())
        fixed = max(1, used // 4)
        moved = fixed + (places - fixed + turn * (used - fixed)) % max(1, number_of - fixed)
        return jnp.zeros((number_of,), jnp.int32).at[order[jnp.where(places < fixed, places, moved)]].set(jnp.asarray(lengths, jnp.int32))

    lengths = jnp.where(number % 4 == 0, named(crowded, number // 4), named(common, number - number // 4 - 1))
    mixed = jax.random.permutation(jax.random.fold_in(own, 3), number_of)
    source_of, sink = mixed[0:number_of // 2 * 2:2], mixed[1:number_of // 2 * 2:2]
    room = jnp.minimum(lengths[source_of] - 1, limit - lengths[sink]) // 2
    room = jnp.where((source_of == order[0]) | (sink == order[0]) | (lengths[sink] == 0), 0, jnp.maximum(room, 0))
    moved = jax.random.randint(jax.random.fold_in(own, 4), (number_of // 2,), 0, 1 << 20) % (room + 1)
    lengths = lengths.at[source_of].add(-moved).at[sink].add(moved)
    items = jnp.searchsorted(jnp.cumsum(lengths), jnp.arange(rows * top), side="right").astype(jnp.int32)
    table = items.reshape(top, rows).T
    table = table[jax.random.permutation(jax.random.fold_in(own, 1), rows)]
    turn = jax.random.randint(jax.random.fold_in(own, 2), (rows, 1), 0, top)
    return jnp.take_along_axis(table, (jnp.arange(top)[None, :] + turn) % top, axis=1)


def portions_of(count, total, bound, lean, full):
    weights = [(1 << 20) // math.isqrt(grade ** lean) + 1 for grade in range(1, count + 1)]
    largest = bound if full else min(bound, max(-(-total // count), total * weights[0] // sum(weights)))
    least = 1 if total - largest >= count - 1 else 0
    given, rest = [largest] + [least] * (count - 1), total - largest - least * (count - 1)
    while rest > 0:
        candidates = [i for i in range(1, count) if given[i] < largest] or [i for i in range(1, count) if given[i] < bound]
        mass, left = sum([weights[i] for i in candidates]), rest
        for i in candidates:
            more = min(bound - given[i], max(1, left * weights[i] // mass), rest)
            given[i] = given[i] + more
            rest = rest - more
    return np.array(given)


def gaussian(rng, dims, scale, most, split=(), kind=jnp.bfloat16):
    result = scale * jax.random.normal(rng, dims, jnp.float32)
    if split:
        result = result * shard_levels(rng, dims, split, -0.22, 0.18)
    return jnp.clip(result, -most, most).astype(kind)


def setup_inputs(seed: int = 0, part: int = 0) -> dict:
    splits = jax.random.split(jax.random.key(seed), 16)
    part_splits = jax.random.split(jax.random.fold_in(splits[15], part), 16)
    eta_c = gaussian(part_splits[0], (NYC, CX), 0.5, 4.0, ((0, 16),), jnp.float32)
    u_c = gaussian(part_splits[1], (NYC, CX), 0.5, 4.0, ((0, 16),), jnp.float32)
    v_c = gaussian(part_splits[2], (NYC, CX), 0.5, 4.0, ((0, 16),), jnp.float32)
    depth_c = jnp.clip(0.2 + 0.8 * jax.random.uniform(part_splits[3], (NYC, CX), jnp.float32) ** shard_levels(part_splits[3], (NYC, CX), ((0, 16),), -0.2, 0.2), 0.2, 1.0)
    eta_f = gaussian(part_splits[4], (NYF, FX), 0.5, 4.0, ((0, 16),), jnp.float32)
    u_f = gaussian(part_splits[5], (NYF, FX), 0.5, 4.0, ((0, 16),), jnp.float32)
    v_f = gaussian(part_splits[6], (NYF, FX), 0.5, 4.0, ((0, 16),), jnp.float32)
    wet_f = plant((jax.random.randint(part_splits[7], (NYF, FX), 0, 5) < 4).astype(jnp.int32), jax.random.fold_in(part_splits[7], 1), 0, 1)
    topography = jnp.clip(0.2 + 0.8 * jax.random.uniform(part_splits[8], (DEV * TB, FP, FX), jnp.float32) ** shard_levels(part_splits[8], (DEV * TB, FP, FX), ((0, 16),), -0.2, 0.2), 0.2, 1.0)
    owner_list_keys = jax.random.split(jax.random.fold_in(part_splits[9], 1), (DEV * NP) // NP)
    owner_list_turns = jax.random.permutation(jax.random.fold_in(part_splits[9], 3), (DEV * NP) // NP)
    owner_list = jax.vmap(lambda own, number: shared_out(jax.random.fold_in(part_splits[9], 2), own, number, NP, N_PATCH, 1, CAP, 2))(owner_list_keys, owner_list_turns).reshape((DEV * NP, 1))
    block_list = plant(jax.random.randint(part_splits[10], (DEV * NP,), 0, TB), jax.random.fold_in(part_splits[10], 1), 0, TB - 1).astype(jnp.int32)
    fault_row = jnp.clip(3072.0 * jax.random.uniform(part_splits[11], (NF,), jnp.float32) ** shard_levels(part_splits[11], (NF,), ((0, 16),), -0.2, 0.2), 0.0, 3072.0)
    fault_col = jnp.clip(768.0 * jax.random.uniform(part_splits[12], (NF,), jnp.float32) ** shard_levels(part_splits[12], (NF,), ((0, 16),), -0.2, 0.2), 0.0, 768.0)
    fault_width = jnp.clip(3.0 + 9.0 * jax.random.uniform(part_splits[13], (NF,), jnp.float32) ** shard_levels(part_splits[13], (NF,), ((0, 16),), -0.2, 0.2), 3.0, 12.0)
    fault_slip = gaussian(part_splits[14], (NF,), 1.0, 5.0, ((0, 16),), jnp.float32)
    return {"eta_c": eta_c, "u_c": u_c, "v_c": v_c, "depth_c": depth_c, "eta_f": eta_f, "u_f": u_f, "v_f": v_f, "wet_f": wet_f, "topography": topography, "owner_list": owner_list, "block_list": block_list, "fault_row": fault_row, "fault_col": fault_col, "fault_width": fault_width, "fault_slip": fault_slip}


courant = 0.35


def fault_block(first_row, fault_row, fault_col, fault_width, fault_slip):
    rows_idx = first_row + jnp.arange(CY, dtype=jnp.float32)
    cols_idx = jnp.arange(CX, dtype=jnp.float32)
    along_y = (rows_idx[:, None] - fault_row[None, :]) / fault_width[None, :]
    along = jnp.exp(-along_y * along_y) * fault_slip[None, :]
    across_x = (cols_idx[None, :] - fault_col[:, None]) / fault_width[:, None]
    across = (1.0 + across_x) * jnp.exp(-across_x * across_x)
    return jnp.dot(along, across, precision=lax.Precision.HIGHEST, preferred_element_type=jnp.float32)


def advance(eta, u, v, depth, wet, ghost, west_open):
    rows = eta.shape[0]
    cols = eta.shape[1]
    zero_col = jnp.zeros((rows, 1), jnp.float32)
    zero_row = jnp.zeros((1, cols), jnp.float32)
    eta_west = jnp.concatenate([ghost[:, None], eta[:, :-1]], 1)
    h_west = jnp.concatenate([depth[:, :1], 0.5 * (depth[:, :-1] + depth[:, 1:])], 1)
    m_west = jnp.concatenate([wet[:, :1] * west_open, wet[:, :-1] * wet[:, 1:]], 1)
    u_new = (u - courant * (eta - eta_west)) * m_west
    flux_x = h_west * u_new
    flux_east = jnp.concatenate([flux_x[:, 1:], zero_col], 1)
    eta_south = jnp.concatenate([zero_row, eta[:-1]], 0)
    h_south = jnp.concatenate([zero_row, depth[:-1]], 0)
    m_south = jnp.concatenate([zero_row, wet[:-1]], 0)
    v_new = (v - courant * (eta - eta_south)) * wet * m_south
    flux_y = 0.5 * (depth + h_south) * v_new
    flux_north = jnp.concatenate([flux_y[1:], zero_row], 0)
    eta_new = eta - courant * (flux_east - flux_x + flux_north - flux_y)
    return eta_new, u_new, v_new


def reference(eta_c, u_c, v_c, depth_c, eta_f, u_f, v_f, wet_f, topography, owner_list, block_list, fault_row, fault_col, fault_width, fault_slip):
    starts = jnp.arange(DEV, dtype=jnp.float32) * CY
    uplift = lax.map(lambda first: fault_block(first, fault_row, fault_col, fault_width, fault_slip), starts).reshape(NYC, CX)
    index = jnp.arange(DEV * NP, dtype=jnp.int32)
    device = index // NP
    source = owner_list[:, 0] * N_SUB + device % N_SUB
    depth_f = topography[source * TB + block_list].reshape(NYF, FX)
    eta_start = eta_c + uplift
    ones_c = jnp.ones((NYC, CX), jnp.float32)
    zero_ghost = jnp.zeros((NYC,), jnp.float32)
    eta_c1, u_c1, v_c1 = advance(eta_start, u_c, v_c, depth_c, ones_c, zero_ghost, 0.0)
    first_col = CX - FX // 2
    fine_uplift = jnp.repeat(jnp.repeat(uplift[:, first_col:], 2, 0), 2, 1)
    ghost_old = jnp.repeat(eta_start[:, first_col - 1], 2)
    ghost_new = jnp.repeat(eta_c1[:, first_col - 1], 2)
    wet = wet_f.astype(jnp.float32)
    eta, u, v = eta_f + fine_uplift, u_f, v_f
    for step in range(2):
        ghost = ghost_old + (step + 1) / 2.0 * (ghost_new - ghost_old)
        eta, u, v = advance(eta, u, v, depth_f, wet, ghost, 1.0)
    return eta_c1, u_c1, v_c1, eta, u, v
```

```python
import functools

import jax
import jax.numpy as jnp
from jax import lax
from jax.experimental import pallas as pl
from jax.experimental.pallas import tpu as pltpu
from jax.sharding import PartitionSpec as P

FP = 2
LANES = 128
PAD = 16
HALO = 8
CH = 16
KB = 256
PARTS = 2

courant = 0.35


def west(x):
    return pltpu.roll(x, 1, 1)


def east(x):
    return pltpu.roll(x, x.shape[1] - 1, 1)


def south_of(ref, b, here):
    edge = ref[pl.ds(pl.multiple_of(b - 8, 8), 8)]
    return pltpu.roll(jnp.concatenate([edge, here], 0), 1, 0)[8:]


def north_of(ref, b, here):
    edge = ref[pl.ds(pl.multiple_of(b + CH, 8), 8)]
    return pltpu.roll(jnp.concatenate([here, edge], 0), CH + 7, 0)[:CH]


def ring_position(p, n):
    odd = p % 2
    return (1 - odd) * (p // 2) + odd * (n - 1 - p // 2)


def ring_patch(k, n):
    back = k // (n // 2)
    return (1 - back) * (2 * k) + back * (2 * (n - 1 - k) + 1)


def kernel(
    n_patch,
    n_sub,
    src_ref,
    faults_ref,
    eta_c_in,
    u_c_in,
    v_c_in,
    depth_c_in,
    eta_f_in,
    u_f_in,
    v_f_in,
    wet_f_in,
    topo_in,
    eta_c_out,
    u_c_out,
    v_c_out,
    eta_f_out,
    u_f_out,
    v_f_out,
    gath,
    fbuf,
    fpar,
    etac,
    uc,
    vc,
    hc,
    gc,
    etac1,
    etaf,
    uf,
    vf,
    wetf,
    wet,
    mwf,
    mmf,
    hf,
    hwf,
    hsf,
    gf,
    etap,
    ghost1,
    ghost2,
    local_sem,
    out_sem,
    ring_send,
    ring_recv,
    fault_send,
    fault_recv,
    halo_send,
    halo_recv,
    rim_send,
    rim_recv,
):
    mesh_id = pl.DeviceIdType.MESH
    patch = lax.axis_index("patch")
    sub = lax.axis_index("sub")
    n = n_patch * n_sub
    me = patch * n_sub + sub
    rows_c, cols_c = eta_c_in.shape
    rows_f, cols_f = eta_f_in.shape
    held = topo_in.shape[0]
    first_col = cols_c - cols_f // 2

    def where(flat):
        return {"patch": flat // n_sub, "sub": flat % n_sub}

    own_topo = pltpu.make_async_copy(
        topo_in, gath.at[pl.ds(patch * held, held)], local_sem.at[8]
    )
    own_topo.start()
    pairs = [
        (eta_c_in, etac),
        (u_c_in, uc),
        (v_c_in, vc),
        (depth_c_in, hc),
        (eta_f_in, etaf),
        (u_f_in, uf),
        (v_f_in, vf),
        (wet_f_in, wet),
    ]
    loads = []
    for i, (src, dst) in enumerate(pairs):
        copy = pltpu.make_async_copy(
            src, dst.at[pl.ds(PAD, src.shape[0])], local_sem.at[i]
        )
        copy.start()
        loads.append(copy)

    barrier = pltpu.get_barrier_semaphore()

    def greet(i, carry):
        pl.semaphore_signal(
            barrier, inc=1, device_id=where((me + i) % n), device_id_type=mesh_id
        )
        return carry

    lax.fori_loop(1, n, greet, 0)
    for ref in (etac, hc, gc, etac1, etaf, hf, gf, wet, etap):
        rows = ref.shape[0]
        zero = jnp.zeros((PAD - HALO, ref.shape[1]), ref.dtype)
        ref[0 : PAD - HALO] = zero
        ref[rows - (PAD - HALO) : rows] = zero
    pl.semaphore_wait(barrier, n - 1)

    here = ring_position(patch, n_patch)
    following = ring_patch((here + 1) % n_patch, n_patch)
    before = ring_patch((here + n_patch - 1) % n_patch, n_patch)
    piece = held // (2 * PARTS)

    def ring_copy(way, part, step):
        if way == 0:
            owner = ring_patch((here + n_patch - step) % n_patch, n_patch)
            target = following
        else:
            owner = ring_patch((here + step) % n_patch, n_patch)
            target = before
        block = gath.at[pl.ds(owner * held + (way * PARTS + part) * piece, piece)]
        index = (way * PARTS + part) * (n_patch - 1) + step
        return pltpu.make_async_remote_copy(
            src_ref=block,
            dst_ref=block,
            send_sem=ring_send.at[index],
            recv_sem=ring_recv.at[index],
            device_id={"patch": target, "sub": sub},
            device_id_type=mesh_id,
        )

    def ring_step(step, part):
        for way in (0, 1):
            ring_copy(way, part, step - 1).wait_recv()
            ring_copy(way, part, step).start()

    own_topo.wait()
    for part in range(PARTS):
        for way in (0, 1):
            ring_copy(way, part, 0).start()

    def fault_copy(i):
        return pltpu.make_async_remote_copy(
            src_ref=faults_ref,
            dst_ref=fbuf.at[me],
            send_sem=fault_send.at[i - 1],
            recv_sem=fault_recv.at[i - 1],
            device_id=where((me + i) % n),
            device_id_type=mesh_id,
        )

    def send_fault(i, carry):
        fault_copy(i).start()
        return carry

    lax.fori_loop(1, n, send_fault, 0)

    halos = []
    north, south = where((me + 1) % n), where((me + n - 1) % n)
    for i, (src, dst) in enumerate(pairs):
        rows = src.shape[0]
        up = pltpu.make_async_remote_copy(
            src_ref=src.at[pl.ds(rows - HALO, HALO)],
            dst_ref=dst.at[pl.ds(PAD - HALO, HALO)],
            send_sem=halo_send.at[2 * i],
            recv_sem=halo_recv.at[2 * i],
            device_id=north,
            device_id_type=mesh_id,
        )
        down = pltpu.make_async_remote_copy(
            src_ref=src.at[pl.ds(0, HALO)],
            dst_ref=dst.at[pl.ds(PAD + rows, HALO)],
            send_sem=halo_send.at[2 * i + 1],
            recv_sem=halo_recv.at[2 * i + 1],
            device_id=south,
            device_id_type=mesh_id,
        )
        up.start()
        down.start()
        halos.append((up, down))

    def arrived(indices):
        for i in indices:
            loads[i].wait()
            for copy in halos[i]:
                copy.wait_recv()

    def gather_faults():
        fbuf[me] = faults_ref[...]

        def wait_fault(i, carry):
            fault_copy(i).wait_recv()
            return carry

        lax.fori_loop(1, n, wait_fault, 0)
        per_tile = n * LANES // fpar.shape[1]
        for t in range(fpar.shape[1] // LANES):
            fpar[:, t * LANES : (t + 1) * LANES] = jnp.sum(
                fbuf[t * per_tile : (t + 1) * per_tile], axis=0
            )

    def add_uplift(eta, rows_at, cols_at):
        total = eta.shape[0]
        width = eta.shape[1]

        def block(kb, carry):
            at = pl.ds(pl.multiple_of(kb * KB, KB), KB)
            centre_row = fpar[0:1, at]
            centre_col = fpar[1:2, at]
            widths = fpar[2:3, at]
            slips = fpar[3:4, at]
            y = rows_at(lax.broadcasted_iota(jnp.int32, (total, KB), 0))
            along_y = (y.astype(jnp.float32) - centre_row) / widths
            along = jnp.exp(-along_y * along_y) * slips
            x = cols_at(lax.broadcasted_iota(jnp.int32, (width, KB), 0))
            across_x = (x.astype(jnp.float32) - centre_col) / widths
            across = (1.0 + across_x) * jnp.exp(-across_x * across_x)
            eta[...] += lax.dot_general(
                along,
                across,
                (((1,), (1,)), ((), ())),
                precision=lax.Precision.HIGHEST,
                preferred_element_type=jnp.float32,
            )
            return carry

        if fpar.shape[1] == KB:
            block(0, 0)
        else:
            lax.fori_loop(0, fpar.shape[1] // KB, block, 0)

    def coarse_uplift():
        arrived([0])
        add_uplift(etac, lambda i: me * rows_c + i - PAD, lambda i: i)

    def fine_uplift():
        arrived([4])
        add_uplift(
            etaf, lambda i: me * rows_c + i // 2 - PAD // 2, lambda i: first_col + i // 2
        )

    def chunks(body, first, last):
        def step(i, carry):
            body(pl.multiple_of(first + i * CH, 8))
            return carry

        lax.fori_loop(0, (last - first) // CH, step, 0)

    lo_c, hi_c = PAD - HALO, PAD + rows_c + HALO
    lo_f, hi_f = PAD - HALO, PAD + rows_f + HALO

    def coarse_faces():
        arrived([1, 2, 3])

        def body(b):
            at = pl.ds(pl.multiple_of(b, 8), CH)
            col = lax.broadcasted_iota(jnp.int32, (CH, cols_c), 1)
            row = lax.broadcasted_iota(jnp.int32, (CH, cols_c), 0) + (
                me * rows_c + b - PAD
            )
            eta, h = etac[at], hc[at]
            u = jnp.where(col > 0, uc[at] - courant * (eta - west(eta)), 0.0)
            flux_x = 0.5 * (h + west(h)) * u
            v = vc[at] - courant * (eta - south_of(etac, b, eta))
            v = jnp.where((row >= 1) & (row < n * rows_c), v, 0.0)
            flux_y = 0.5 * (h + south_of(hc, b, h)) * v
            uc[at] = u
            vc[at] = v
            gc[at] = flux_y
            etac1[at] = eta - courant * (east(flux_x) - flux_x - flux_y)

        chunks(body, lo_c, hi_c)

    outs = []

    def write(src, dst):
        copy = pltpu.make_async_copy(
            src.at[pl.ds(PAD, dst.shape[0])], dst, out_sem.at[len(outs)]
        )
        copy.start()
        outs.append(copy)

    def coarse_eta():
        def body(b):
            at = pl.ds(pl.multiple_of(b, 8), CH)
            etac1[at] = etac1[at] - courant * north_of(gc, b, gc[at])

        chunks(body, lo_c, hi_c)
        write(etac1, eta_c_out)
        write(uc, u_c_out)
        write(vc, v_c_out)

    def ghosts():
        rows = ghost1.shape[0]
        coarse = lax.broadcasted_iota(jnp.int32, (rows, etac.shape[0]), 1)
        fine = lax.broadcasted_iota(jnp.int32, (rows, etac.shape[0]), 0)
        spread = (coarse == fine // 2 + PAD // 2).astype(jnp.float32)
        old = etac[:, first_col - LANES : first_col]
        new = etac1[:, first_col - LANES : first_col]
        for ref, value in ((ghost1, old + 0.5 * (new - old)), (ghost2, new)):
            ref[...] = west(
                jnp.dot(
                    spread,
                    value,
                    precision=lax.Precision.HIGHEST,
                    preferred_element_type=jnp.float32,
                )
            )

    def eta_west(eta, ghost, col):
        return jnp.where(
            col == 0, jnp.concatenate([ghost] * (cols_f // LANES), 1), west(eta)
        )

    def fine_masks():
        arrived([5, 6, 7])
        wet[lo_f:PAD] = wet[lo_f:PAD] * (me + n - 1) // n
        wet[PAD + rows_f : hi_f] = wet[PAD + rows_f : hi_f] * (
            (2 * n - 2 - me) // n
        )
        wetf[...] = wet[...].astype(jnp.float32)

    def fine_first():
        def body(b):
            at = pl.ds(pl.multiple_of(b, 8), CH)
            col = lax.broadcasted_iota(jnp.int32, (CH, cols_f), 1)
            m = wetf[at]
            mw = m * jnp.where(col == 0, 1.0, west(m))
            mm = m * south_of(wetf, b, m)
            eta = etaf[at]
            mwf[at] = mw
            mmf[at] = mm
            uf[at] = (uf[at] - courant * (eta - eta_west(eta, ghost1[at], col))) * mw
            vf[at] = (vf[at] - courant * (eta - south_of(etaf, b, eta))) * mm

        chunks(body, lo_f, hi_f)

    work = [
        gather_faults,
        coarse_uplift,
        coarse_faces,
        coarse_eta,
        ghosts,
        fine_uplift,
        fine_masks,
        fine_first,
    ]
    shown = min(n_patch - 1, 7)
    for step in range(1, shown):
        for part in range(PARTS):
            if work:
                work.pop(0)()
            ring_step(step, part)
    for piece_of_work in work:
        piece_of_work()
    if shown < n_patch - 1:

        def later(step, carry):
            for part in range(PARTS):
                ring_step(step, part)
            return carry

        lax.fori_loop(shown, n_patch - 1, later, 0)
    for part in range(PARTS):
        for way in (0, 1):
            ring_copy(way, part, n_patch - 2).wait_recv()

    def take(i, carry):
        blocks = [gath[src_ref[i * 4 + j]] for j in range(4)]
        row = pl.multiple_of(PAD + i * 8, 8)
        for t in range(cols_f // LANES):
            hf[pl.ds(row, 8), t * LANES : (t + 1) * LANES] = jnp.concatenate(
                [b[t * FP : (t + 1) * FP] for b in blocks], 0
            )
        return carry

    lax.fori_loop(0, rows_f // 8, take, 0)
    rims = []
    for i, (first, to, target) in enumerate(
        ((PAD + rows_f - HALO, PAD - HALO, north), (PAD, PAD + rows_f, south))
    ):
        copy = pltpu.make_async_remote_copy(
            src_ref=hf.at[pl.ds(first, HALO)],
            dst_ref=hf.at[pl.ds(to, HALO)],
            send_sem=rim_send.at[i],
            recv_sem=rim_recv.at[i],
            device_id=target,
            device_id_type=mesh_id,
        )
        copy.start()
        rims.append(copy)
    for copy in rims:
        copy.wait()

    def fine_flux(b):
        at = pl.ds(pl.multiple_of(b, 8), CH)
        col = lax.broadcasted_iota(jnp.int32, (CH, cols_f), 1)
        h = hf[at]
        hw = jnp.where(col == 0, h, 0.5 * (h + west(h)))
        hs = 0.5 * (h + south_of(hf, b, h))
        flux_x = hw * uf[at]
        flux_y = hs * vf[at]
        hwf[at] = hw
        hsf[at] = hs
        gf[at] = flux_y
        flux_east = jnp.where(col == cols_f - 1, 0.0, east(flux_x))
        etaf[at] = etaf[at] - courant * (flux_east - flux_x - flux_y)

    chunks(fine_flux, lo_f, hi_f)

    def fine_eta(b):
        at = pl.ds(pl.multiple_of(b, 8), CH)
        etaf[at] = etaf[at] - courant * north_of(gf, b, gf[at])

    chunks(fine_eta, lo_f, hi_f)

    def fine_second(b):
        at = pl.ds(pl.multiple_of(b, 8), CH)
        col = lax.broadcasted_iota(jnp.int32, (CH, cols_f), 1)
        eta = etaf[at]
        u = (uf[at] - courant * (eta - eta_west(eta, ghost2[at], col))) * mwf[at]
        v = (vf[at] - courant * (eta - south_of(etaf, b, eta))) * mmf[at]
        flux_x = hwf[at] * u
        flux_y = hsf[at] * v
        uf[at] = u
        vf[at] = v
        gf[at] = flux_y
        flux_east = jnp.where(col == cols_f - 1, 0.0, east(flux_x))
        etap[at] = eta - courant * (flux_east - flux_x - flux_y)

    chunks(fine_second, lo_f, hi_f)
    write(uf, u_f_out)
    write(vf, v_f_out)

    def fine_last(b):
        at = pl.ds(pl.multiple_of(b, 8), CH)
        etap[at] = etap[at] - courant * north_of(gf, b, gf[at])

    chunks(fine_last, PAD, PAD + rows_f)
    write(etap, eta_f_out)

    def sent(i, carry):
        fault_copy(i).wait_send()
        return carry

    lax.fori_loop(1, n, sent, 0)
    for up, down in halos:
        up.wait_send()
        down.wait_send()

    def passed(step, carry):
        for part in range(PARTS):
            for way in (0, 1):
                ring_copy(way, part, step).wait_send()
        return carry

    lax.fori_loop(0, n_patch - 1, passed, 0)
    for copy in outs:
        copy.wait()


def on_device(
    eta_c,
    u_c,
    v_c,
    depth_c,
    eta_f,
    u_f,
    v_f,
    wet_f,
    topography,
    owner_list,
    block_list,
    fault_row,
    fault_col,
    fault_width,
    fault_slip,
):
    rows_c, cols_c = eta_c.shape
    rows_f, cols_f = eta_f.shape
    n_patch = lax.axis_size("patch")
    n_sub = lax.axis_size("sub")
    n = n_patch * n_sub
    count = rows_f // FP
    held = topography.shape[0]
    mine = fault_row.shape[0]
    device = lax.axis_index(("patch", "sub"))
    source = lax.dynamic_slice_in_dim(
        owner_list[:, 0], device * count, count
    ) * held + lax.dynamic_slice_in_dim(block_list, device * count, count)
    per_tile = LANES // mine
    params = jnp.stack([fault_row, fault_col, fault_width, fault_slip])
    lane = jnp.arange(LANES) // mine
    faults = jnp.where(
        lane[None, :] == device % per_tile, jnp.tile(params, (2, per_tile)), 0.0
    )
    tiles = (
        topography.reshape(held, FP, cols_f // LANES, LANES)
        .transpose(0, 2, 1, 3)
        .reshape(held, FP * cols_f // LANES, LANES)
    )
    f32 = jnp.float32
    coarse = pltpu.VMEM((rows_c + 2 * PAD, cols_c), f32)
    fine = pltpu.VMEM((rows_f + 2 * PAD, cols_f), f32)
    dma = pltpu.SemaphoreType.DMA
    any_spec = pl.BlockSpec(memory_space=pl.ANY)
    return pl.pallas_call(
        functools.partial(kernel, n_patch, n_sub),
        out_shape=[jax.ShapeDtypeStruct((rows_c, cols_c), f32)] * 3
        + [jax.ShapeDtypeStruct((rows_f, cols_f), f32)] * 3,
        in_specs=[
            pl.BlockSpec(memory_space=pltpu.SMEM),
            pl.BlockSpec(memory_space=pltpu.VMEM),
        ]
        + [any_spec] * 9,
        out_specs=[any_spec] * 6,
        scratch_shapes=[
            pltpu.VMEM((n_patch * held,) + tiles.shape[1:], f32),
            pltpu.VMEM((n, 8, LANES), f32),
            pltpu.VMEM((8, n * mine), f32),
        ]
        + [coarse] * 6
        + [fine] * 4
        + [pltpu.VMEM((rows_f + 2 * PAD, cols_f), jnp.int32)]
        + [fine] * 7
        + [pltpu.VMEM((rows_f + 2 * PAD, LANES), f32)] * 2
        + [
            dma((9,)),
            dma((6,)),
            dma((2 * PARTS * (n_patch - 1),)),
            dma((2 * PARTS * (n_patch - 1),)),
            dma((n - 1,)),
            dma((n - 1,)),
            dma((16,)),
            dma((16,)),
            dma((2,)),
            dma((2,)),
        ],
        compiler_params=pltpu.CompilerParams(
            collective_id=0, has_side_effects=True, vmem_limit_bytes=60 * 2**20
        ),
    )(
        source,
        faults,
        eta_c,
        u_c,
        v_c,
        depth_c,
        eta_f,
        u_f,
        v_f,
        wet_f,
        tiles,
    )


def solution(mesh):
    rows = P(("runs", "patch", "sub"), None)
    line = P(("runs", "patch", "sub"))
    return jax.shard_map(
        on_device,
        mesh=mesh,
        in_specs=(rows,) * 8
        + (P(("runs", "patch", "sub"), None, None), P("runs", None), P("runs"))
        + (line,) * 4,
        out_specs=(rows,) * 6,
        check_vma=False,
    )
```

```python
import functools

import jax
import jax.numpy as jnp
from jax import lax
from jax.experimental import pallas as pl
from jax.experimental.pallas import tpu as pltpu
from jax.sharding import PartitionSpec as P

FP = 2
LANES = 128
PAD = 16
HALO = 8
CH = 16
KB = 256
PARTS = 2
SLABS = 2

courant = 0.35


def west(x):
    return pltpu.roll(x, 1, 1)


def east(x):
    return pltpu.roll(x, x.shape[1] - 1, 1)


def south_of(ref, b, here):
    edge = ref[pl.ds(pl.multiple_of(b - 8, 8), 8)]
    return pltpu.roll(jnp.concatenate([edge, here], 0), 1, 0)[8:]


def north_of(here, above):
    rows = here.shape[0]
    return pltpu.roll(jnp.concatenate([here, above], 0), rows + 7, 0)[:rows]


def ring_position(p, n):
    odd = p % 2
    return (1 - odd) * (p // 2) + odd * (n - 1 - p // 2)


def ring_patch(k, n):
    back = k // (n // 2)
    return (1 - back) * (2 * k) + back * (2 * (n - 1 - k) + 1)


def kernel(
    n_patch,
    n_sub,
    owner_in,
    block_in,
    faults_in,
    eta_c_in,
    u_c_in,
    v_c_in,
    depth_c_in,
    eta_f_in,
    u_f_in,
    v_f_in,
    wet_f_in,
    topo_in,
    eta_c_out,
    u_c_out,
    v_c_out,
    eta_f_out,
    u_f_out,
    v_f_out,
    owners,
    blocks,
    faults_ref,
    gath,
    fbuf,
    fpar,
    etac,
    uc,
    vc,
    hc,
    etac1,
    etaf,
    uf,
    vf,
    wetf,
    wet,
    mwf,
    mmf,
    hf,
    hwf,
    hsf,
    etap,
    rim,
    ghost1,
    ghost2,
    local_sem,
    out_sem,
    ring_send,
    ring_recv,
    fault_send,
    fault_recv,
    halo_send,
    halo_recv,
    rim_send,
    rim_recv,
):
    mesh_id = pl.DeviceIdType.MESH
    patch = lax.axis_index("patch")
    sub = lax.axis_index("sub")
    n = n_patch * n_sub
    me = patch * n_sub + sub
    rows_c, cols_c = eta_c_in.shape
    rows_f, cols_f = eta_f_in.shape
    held = topo_in.shape[0]
    first_col = cols_c - cols_f // 2

    def where(flat):
        return {"patch": flat // n_sub, "sub": flat % n_sub}

    own_topo = pltpu.make_async_copy(
        topo_in, gath.at[pl.ds(patch * held, held)], local_sem.at[8]
    )
    own_topo.start()
    pairs = [
        (eta_c_in, etac),
        (u_c_in, uc),
        (v_c_in, vc),
        (depth_c_in, hc),
        (eta_f_in, etaf),
        (u_f_in, uf),
        (v_f_in, vf),
        (wet_f_in, wet),
    ]
    loads = []
    for i, (src, dst) in enumerate(pairs):
        copy = pltpu.make_async_copy(
            src, dst.at[pl.ds(PAD, src.shape[0])], local_sem.at[i]
        )
        copy.start()
        loads.append(copy)

    lists = []
    for i, (src, dst) in enumerate(((owner_in, owners), (block_in, blocks))):
        copy = pltpu.make_async_copy(src, dst, local_sem.at[9 + i])
        copy.start()
        lists.append(copy)

    barrier = pltpu.get_barrier_semaphore()

    def greet(i, carry):
        pl.semaphore_signal(
            barrier, inc=1, device_id=where((me + i) % n), device_id_type=mesh_id
        )
        return carry

    lax.fori_loop(1, n, greet, 0)
    per_tile = LANES * n // fpar.shape[1]
    faults_ref[...] = pltpu.roll(
        faults_in[...], (me % per_tile) * (LANES // per_tile), 1
    )
    for ref in (etac, hc, etac1, etaf, hf, wet):
        rows = ref.shape[0]
        zero = jnp.zeros((PAD - HALO, ref.shape[1]), ref.dtype)
        ref[0 : PAD - HALO] = zero
        ref[rows - (PAD - HALO) : rows] = zero
    pl.semaphore_wait(barrier, n - 1)

    here = ring_position(patch, n_patch)
    following = ring_patch((here + 1) % n_patch, n_patch)
    before = ring_patch((here + n_patch - 1) % n_patch, n_patch)
    piece = held // (2 * PARTS)

    def ring_copy(way, part, step):
        if way == 0:
            owner = ring_patch((here + n_patch - step) % n_patch, n_patch)
            target = following
        else:
            owner = ring_patch((here + step) % n_patch, n_patch)
            target = before
        block = gath.at[pl.ds(owner * held + (way * PARTS + part) * piece, piece)]
        index = (way * PARTS + part) * (n_patch - 1) + step
        return pltpu.make_async_remote_copy(
            src_ref=block,
            dst_ref=block,
            send_sem=ring_send.at[index],
            recv_sem=ring_recv.at[index],
            device_id={"patch": target, "sub": sub},
            device_id_type=mesh_id,
        )

    def ring_step(step, part):
        for way in (0, 1):
            ring_copy(way, part, step - 1).wait_recv()
            ring_copy(way, part, step).start()

    own_topo.wait()
    for part in range(PARTS):
        for way in (0, 1):
            ring_copy(way, part, 0).start()

    def fault_copy(i):
        return pltpu.make_async_remote_copy(
            src_ref=faults_ref,
            dst_ref=fbuf.at[me],
            send_sem=fault_send.at[i - 1],
            recv_sem=fault_recv.at[i - 1],
            device_id=where((me + i) % n),
            device_id_type=mesh_id,
        )

    def send_fault(i, carry):
        fault_copy(i).start()
        return carry

    lax.fori_loop(1, n, send_fault, 0)

    halos = []
    north, south = where((me + 1) % n), where((me + n - 1) % n)
    for i, (src, dst) in enumerate(pairs):
        rows = src.shape[0]
        up = pltpu.make_async_remote_copy(
            src_ref=src.at[pl.ds(rows - HALO, HALO)],
            dst_ref=dst.at[pl.ds(PAD - HALO, HALO)],
            send_sem=halo_send.at[2 * i],
            recv_sem=halo_recv.at[2 * i],
            device_id=north,
            device_id_type=mesh_id,
        )
        down = pltpu.make_async_remote_copy(
            src_ref=src.at[pl.ds(0, HALO)],
            dst_ref=dst.at[pl.ds(PAD + rows, HALO)],
            send_sem=halo_send.at[2 * i + 1],
            recv_sem=halo_recv.at[2 * i + 1],
            device_id=south,
            device_id_type=mesh_id,
        )
        up.start()
        down.start()
        halos.append((up, down))

    def arrived(indices):
        for i in indices:
            loads[i].wait()
            for copy in halos[i]:
                copy.wait_recv()

    def gather_faults():
        fbuf[me] = faults_ref[...]

        def wait_fault(i, carry):
            fault_copy(i).wait_recv()
            return carry

        lax.fori_loop(1, n, wait_fault, 0)
        for t in range(fpar.shape[1] // LANES):
            fpar[:, t * LANES : (t + 1) * LANES] = jnp.sum(
                fbuf[t * per_tile : (t + 1) * per_tile], axis=0
            )

    def add_uplift(eta, rows_at, cols_at):
        total = eta.shape[0]
        width = eta.shape[1]

        def block(kb, carry):
            at = pl.ds(pl.multiple_of(kb * KB, KB), KB)
            centre_row = fpar[0:1, at]
            centre_col = fpar[1:2, at]
            widths = fpar[2:3, at]
            slips = fpar[3:4, at]
            y = rows_at(lax.broadcasted_iota(jnp.int32, (total, KB), 0))
            along_y = (y.astype(jnp.float32) - centre_row) / widths
            along = jnp.exp(-along_y * along_y) * slips
            x = cols_at(lax.broadcasted_iota(jnp.int32, (width, KB), 0))
            across_x = (x.astype(jnp.float32) - centre_col) / widths
            across = (1.0 + across_x) * jnp.exp(-across_x * across_x)
            eta[...] += lax.dot_general(
                along,
                across,
                (((1,), (1,)), ((), ())),
                precision=lax.Precision.HIGHEST,
                preferred_element_type=jnp.float32,
            )
            return carry

        if fpar.shape[1] == KB:
            block(0, 0)
        else:
            lax.fori_loop(0, fpar.shape[1] // KB, block, 0)

    def coarse_uplift():
        arrived([0])
        add_uplift(etac, lambda i: me * rows_c + i - PAD, lambda i: i)

    def fine_uplift():
        arrived([4])
        add_uplift(
            etaf, lambda i: me * rows_c + i // 2 - PAD // 2, lambda i: first_col + i // 2
        )

    def chunks(body, first, last, cols):
        count = (last - first) // CH

        def step(i, carry):
            return body(pl.multiple_of(first + (count - 1 - i) * CH, 8), carry)

        lax.fori_loop(0, count, step, jnp.zeros((8, cols), jnp.float32))

    lo_c, hi_c = PAD - HALO, PAD + rows_c + HALO
    lo_f, hi_f = PAD - HALO, PAD + rows_f + HALO

    def coarse_step():
        arrived([1, 2, 3])

        def body(b, flux_above):
            at = pl.ds(b, CH)
            col = lax.broadcasted_iota(jnp.int32, (CH, cols_c), 1)
            row = lax.broadcasted_iota(jnp.int32, (CH, cols_c), 0) + (
                me * rows_c + b - PAD
            )
            eta, h = etac[at], hc[at]
            u = jnp.where(col > 0, uc[at] - courant * (eta - west(eta)), 0.0)
            flux_x = 0.5 * (h + west(h)) * u
            v = vc[at] - courant * (eta - south_of(etac, b, eta))
            v = jnp.where((row >= 1) & (row < n * rows_c), v, 0.0)
            flux_y = 0.5 * (h + south_of(hc, b, h)) * v
            uc[at] = u
            vc[at] = v
            spread = east(flux_x) - flux_x + north_of(flux_y, flux_above) - flux_y
            etac1[at] = eta - courant * spread
            return flux_y[:8]

        chunks(body, lo_c, hi_c, cols_c)
        write(etac1, eta_c_out)
        write(uc, u_c_out)
        write(vc, v_c_out)

    outs = []

    def write(src, dst):
        copy = pltpu.make_async_copy(
            src.at[pl.ds(PAD, dst.shape[0])], dst, out_sem.at[len(outs)]
        )
        copy.start()
        outs.append(copy)

    def ghosts():
        rows = ghost1.shape[0]
        coarse = lax.broadcasted_iota(jnp.int32, (rows, etac.shape[0]), 1)
        fine = lax.broadcasted_iota(jnp.int32, (rows, etac.shape[0]), 0)
        spread = (coarse == fine // 2 + PAD // 2).astype(jnp.float32)
        old = etac[:, first_col - LANES : first_col]
        new = etac1[:, first_col - LANES : first_col]
        for ref, value in ((ghost1, old + 0.5 * (new - old)), (ghost2, new)):
            ref[...] = west(
                jnp.dot(
                    spread,
                    value,
                    precision=lax.Precision.HIGHEST,
                    preferred_element_type=jnp.float32,
                )
            )

    def eta_west(eta, ghost, col):
        return jnp.where(
            col == 0, jnp.concatenate([ghost] * (cols_f // LANES), 1), west(eta)
        )

    def fine_masks():
        arrived([5, 6, 7])
        wet[lo_f:PAD] = wet[lo_f:PAD] * (me + n - 1) // n
        wet[PAD + rows_f : hi_f] = wet[PAD + rows_f : hi_f] * (
            (2 * n - 2 - me) // n
        )
        wetf[...] = wet[...].astype(jnp.float32)

    def fine_first():
        def body(b, carry):
            at = pl.ds(b, CH)
            col = lax.broadcasted_iota(jnp.int32, (CH, cols_f), 1)
            m = wetf[at]
            mw = m * jnp.where(col == 0, 1.0, west(m))
            mm = m * south_of(wetf, b, m)
            eta = etaf[at]
            mwf[at] = mw
            mmf[at] = mm
            uf[at] = (uf[at] - courant * (eta - eta_west(eta, ghost1[at], col))) * mw
            vf[at] = (vf[at] - courant * (eta - south_of(etaf, b, eta))) * mm
            return carry

        chunks(body, lo_f, hi_f, cols_f)

    work = [
        gather_faults,
        coarse_uplift,
        coarse_step,
        ghosts,
        fine_uplift,
        fine_masks,
        fine_first,
    ]
    shown = min(n_patch - 1, 7)
    for step in range(1, shown):
        for part in range(PARTS):
            if work:
                work.pop(0)()
            ring_step(step, part)
    for piece_of_work in work:
        piece_of_work()
    if shown < n_patch - 1:

        def later(step, carry):
            for part in range(PARTS):
                ring_step(step, part)
            return carry

        lax.fori_loop(shown, n_patch - 1, later, 0)
    for part in range(PARTS):
        for way in (0, 1):
            ring_copy(way, part, n_patch - 2).wait_recv()

    for copy in lists:
        copy.wait()
    count = rows_f // FP

    def take(first, dst, row):
        tiles = [
            gath[owners[first + j] * held + blocks[first + j]] for j in range(4)
        ]
        for t in range(cols_f // LANES):
            dst[pl.ds(row, 8), t * LANES : (t + 1) * LANES] = jnp.concatenate(
                [b[t * FP : (t + 1) * FP] for b in tiles], 0
            )

    mate = patch * n_sub + (n_sub - 1 - sub)
    take((mate * count + n * count - 4) % (n * count), rim, 0)
    take((mate * count + count) % (n * count), rim, 8)
    rims = []
    for i, to in enumerate((PAD - HALO, PAD + rows_f)):
        copy = pltpu.make_async_remote_copy(
            src_ref=rim.at[pl.ds(i * HALO, HALO)],
            dst_ref=hf.at[pl.ds(to, HALO)],
            send_sem=rim_send.at[i],
            recv_sem=rim_recv.at[i],
            device_id={"patch": patch, "sub": n_sub - 1 - sub},
            device_id_type=mesh_id,
        )
        copy.start()
        rims.append(copy)

    def take_own(i, carry):
        take(me * count + i * 4, hf, pl.multiple_of(PAD + i * 8, 8))
        return carry

    lax.fori_loop(0, rows_f // 8, take_own, 0, unroll=4)
    for copy in rims:
        copy.wait()

    def fine_flux(b, flux_above):
        at = pl.ds(b, CH)
        col = lax.broadcasted_iota(jnp.int32, (CH, cols_f), 1)
        h = hf[at]
        hw = jnp.where(col == 0, h, 0.5 * (h + west(h)))
        hs = 0.5 * (h + south_of(hf, b, h))
        flux_x = hw * uf[at]
        flux_y = hs * vf[at]
        hwf[at] = hw
        hsf[at] = hs
        flux_east = jnp.where(col == cols_f - 1, 0.0, east(flux_x))
        spread = flux_east - flux_x + north_of(flux_y, flux_above) - flux_y
        etaf[at] = etaf[at] - courant * spread
        return flux_y[:8]

    chunks(fine_flux, lo_f, hi_f, cols_f)

    def fine_second(b, flux_above):
        at = pl.ds(b, CH)
        col = lax.broadcasted_iota(jnp.int32, (CH, cols_f), 1)
        eta = etaf[at]
        u = (uf[at] - courant * (eta - eta_west(eta, ghost2[at], col))) * mwf[at]
        v = (vf[at] - courant * (eta - south_of(etaf, b, eta))) * mmf[at]
        flux_x = hwf[at] * u
        flux_y = hsf[at] * v
        uf[at] = u
        vf[at] = v
        flux_east = jnp.where(col == cols_f - 1, 0.0, east(flux_x))
        spread = flux_east - flux_x + north_of(flux_y, flux_above) - flux_y
        etap[at] = eta - courant * spread
        return flux_y[:8]

    chunks(fine_second, lo_f, hi_f, cols_f)
    write(uf, u_f_out)
    write(vf, v_f_out)
    write(etap, eta_f_out)

    def sent(i, carry):
        fault_copy(i).wait_send()
        return carry

    lax.fori_loop(1, n, sent, 0)
    for up, down in halos:
        up.wait_send()
        down.wait_send()

    def passed(step, carry):
        for part in range(PARTS):
            for way in (0, 1):
                ring_copy(way, part, step).wait_send()
        return carry

    lax.fori_loop(0, n_patch - 1, passed, 0)
    for copy in outs:
        copy.wait()


def hand_over(*refs):
    results, outputs, staged = refs[:6], refs[6:12], refs[12:18]
    read_sem, write_sem = refs[18:]
    reads, writes = [], []
    for i in (2, 1, 0, 5, 4, 3):
        rows = results[i].shape[0] // SLABS
        for j in range(SLABS):
            at = pl.ds(j * rows, rows)
            k = i * SLABS + j
            reads.append(
                pltpu.make_async_copy(
                    results[i].at[at], staged[i].at[at], read_sem.at[k]
                )
            )
            writes.append(
                pltpu.make_async_copy(
                    staged[i].at[at], outputs[i].at[at], write_sem.at[k]
                )
            )
    for copy in reads:
        copy.start()
    for read, write in zip(reads, writes):
        read.wait()
        write.start()
    for copy in writes:
        copy.wait()


def on_device(
    eta_c,
    u_c,
    v_c,
    depth_c,
    eta_f,
    u_f,
    v_f,
    wet_f,
    topography,
    owner_list,
    block_list,
    fault_row,
    fault_col,
    fault_width,
    fault_slip,
):
    rows_c, cols_c = eta_c.shape
    rows_f, cols_f = eta_f.shape
    n_patch = lax.axis_size("patch")
    n_sub = lax.axis_size("sub")
    n = n_patch * n_sub
    held = topography.shape[0]
    mine = fault_row.shape[0]
    params = jnp.stack([fault_row, fault_col, fault_width, fault_slip])
    faults = jnp.pad(params, ((0, 4), (0, LANES - mine)))
    tiles = (
        topography.reshape(held, FP, cols_f // LANES, LANES)
        .transpose(0, 2, 1, 3)
        .reshape(held, FP * cols_f // LANES, LANES)
    )
    f32 = jnp.float32
    coarse = pltpu.VMEM((rows_c + 2 * PAD, cols_c), f32)
    fine = pltpu.VMEM((rows_f + 2 * PAD, cols_f), f32)
    dma = pltpu.SemaphoreType.DMA
    any_spec = pl.BlockSpec(memory_space=pl.ANY)
    results = pl.pallas_call(
        functools.partial(kernel, n_patch, n_sub),
        out_shape=[jax.ShapeDtypeStruct((rows_c, cols_c), f32)] * 3
        + [jax.ShapeDtypeStruct((rows_f, cols_f), f32)] * 3,
        in_specs=[any_spec] * 2
        + [pl.BlockSpec(memory_space=pltpu.VMEM)]
        + [any_spec] * 9,
        out_specs=[any_spec] * 6,
        scratch_shapes=[
            pltpu.SMEM(block_list.shape, jnp.int32),
            pltpu.SMEM(block_list.shape, jnp.int32),
            pltpu.VMEM((8, LANES), f32),
            pltpu.VMEM((n_patch * held,) + tiles.shape[1:], f32),
            pltpu.VMEM((n, 8, LANES), f32),
            pltpu.VMEM((8, n * mine), f32),
        ]
        + [coarse] * 5
        + [fine] * 4
        + [pltpu.VMEM((rows_f + 2 * PAD, cols_f), jnp.int32)]
        + [fine] * 6
        + [pltpu.VMEM((2 * HALO, cols_f), f32)]
        + [pltpu.VMEM((rows_f + 2 * PAD, LANES), f32)] * 2
        + [
            dma((11,)),
            dma((6,)),
            dma((2 * PARTS * (n_patch - 1),)),
            dma((2 * PARTS * (n_patch - 1),)),
            dma((n - 1,)),
            dma((n - 1,)),
            dma((16,)),
            dma((16,)),
            dma((2,)),
            dma((2,)),
        ],
        compiler_params=pltpu.CompilerParams(
            collective_id=0, has_side_effects=True, vmem_limit_bytes=60 * 2**20
        ),
    )(
        owner_list.reshape(-1),
        block_list,
        faults,
        eta_c,
        u_c,
        v_c,
        depth_c,
        eta_f,
        u_f,
        v_f,
        wet_f,
        tiles,
    )
    return pl.pallas_call(
        hand_over,
        out_shape=[jax.ShapeDtypeStruct(r.shape, r.dtype) for r in results],
        in_specs=[any_spec] * 6,
        out_specs=[any_spec] * 6,
        scratch_shapes=[pltpu.VMEM(r.shape, r.dtype) for r in results]
        + [dma((6 * SLABS,))] * 2,
        compiler_params=pltpu.CompilerParams(vmem_limit_bytes=60 * 2**20),
    )(*results)


def solution(mesh):
    rows = P(("runs", "patch", "sub"), None)
    line = P(("runs", "patch", "sub"))
    return jax.shard_map(
        on_device,
        mesh=mesh,
        in_specs=(rows,) * 8
        + (P(("runs", "patch", "sub"), None, None), P("runs", None), P("runs"))
        + (line,) * 4,
        out_specs=(rows,) * 6,
        check_vma=False,
    )
```

```python
import functools

import jax
import jax.numpy as jnp
from jax import lax
from jax.experimental import pallas as pl
from jax.experimental.pallas import tpu as pltpu
from jax.sharding import PartitionSpec as P

FP = 2
LANES = 128
PAD = 16
HALO = 8
COARSE_CH = 16
FINE_CH = 80
SEGMENTS = 5
KB = 256
PARTS = 2
SLABS = 2

courant = 0.35


def west(x):
    return pltpu.roll(x, 1, 1)


def east(x):
    return pltpu.roll(x, x.shape[1] - 1, 1)


def south_of(ref, b, here):
    edge = ref[pl.ds(pl.multiple_of(b - 8, 8), 8)]
    return pltpu.roll(jnp.concatenate([edge, here], 0), 1, 0)[8:]


def north_of(here, above):
    rows = here.shape[0]
    return pltpu.roll(jnp.concatenate([here, above], 0), rows + 7, 0)[:rows]


def ring_position(p, n):
    odd = p % 2
    return (1 - odd) * (p // 2) + odd * (n - 1 - p // 2)


def ring_patch(k, n):
    back = k // (n // 2)
    return (1 - back) * (2 * k) + back * (2 * (n - 1 - k) + 1)


def kernel(
    n_patch,
    n_sub,
    owner_in,
    block_in,
    row_in,
    col_in,
    width_in,
    slip_in,
    eta_c_in,
    u_c_in,
    v_c_in,
    depth_c_in,
    eta_f_in,
    u_f_in,
    v_f_in,
    wet_f_in,
    topo_in,
    eta_c_out,
    u_c_out,
    v_c_out,
    eta_f_out,
    u_f_out,
    v_f_out,
    owners,
    blocks,
    params,
    faults_ref,
    gath,
    fbuf,
    fpar,
    etac,
    uc,
    vc,
    hc,
    etac1,
    etaf,
    uf,
    vf,
    wetf,
    wet,
    mwf,
    mmf,
    hf,
    hwf,
    hsf,
    etap,
    rim,
    ghost1,
    ghost2,
    local_sem,
    out_sem,
    ring_send,
    ring_recv,
    fault_send,
    fault_recv,
    halo_send,
    halo_recv,
    rim_send,
    rim_recv,
):
    mesh_id = pl.DeviceIdType.MESH
    patch = lax.axis_index("patch")
    sub = lax.axis_index("sub")
    n = n_patch * n_sub
    me = patch * n_sub + sub
    rows_c, cols_c = eta_c_in.shape
    rows_f, cols_f = eta_f_in.shape
    held = topo_in.shape[0]
    first_col = cols_c - cols_f // 2

    def where(flat):
        return {"patch": flat // n_sub, "sub": flat % n_sub}

    own_topo = pltpu.make_async_copy(
        topo_in, gath.at[pl.ds(patch * held, held)], local_sem.at[8]
    )
    own_topo.start()
    pairs = [
        (eta_c_in, etac),
        (u_c_in, uc),
        (v_c_in, vc),
        (depth_c_in, hc),
        (eta_f_in, etaf),
        (u_f_in, uf),
        (v_f_in, vf),
        (wet_f_in, wet),
    ]
    loads = []
    for i, (src, dst) in enumerate(pairs):
        copy = pltpu.make_async_copy(
            src, dst.at[pl.ds(PAD, src.shape[0])], local_sem.at[i]
        )
        copy.start()
        loads.append(copy)

    lists = []
    for i, (src, dst) in enumerate(
        (
            (owner_in, owners),
            (block_in, blocks),
            (row_in, params.at[0]),
            (col_in, params.at[1]),
            (width_in, params.at[2]),
            (slip_in, params.at[3]),
        )
    ):
        copy = pltpu.make_async_copy(src, dst, local_sem.at[9 + i])
        copy.start()
        lists.append(copy)

    barrier = pltpu.get_barrier_semaphore()

    def greet(i, carry):
        pl.semaphore_signal(
            barrier, inc=1, device_id=where((me + i) % n), device_id_type=mesh_id
        )
        return carry

    lax.fori_loop(1, n, greet, 0)
    per_tile = LANES * n // fpar.shape[1]
    for copy in lists[2:]:
        copy.wait()
    line = lax.broadcasted_iota(jnp.int32, (8, LANES), 0)
    lane = lax.broadcasted_iota(jnp.int32, (8, LANES), 1)
    lane = lane - (me % per_tile) * (LANES // per_tile)
    tile = jnp.zeros((8, LANES), jnp.float32)
    for i in range(4):
        for j in range(LANES // per_tile):
            tile = jnp.where((line == i) & (lane == j), params[i, j], tile)
    faults_ref[...] = tile
    for ref in (etac, hc, etac1, etaf, hf, wet):
        rows = ref.shape[0]
        zero = jnp.zeros((PAD - HALO, ref.shape[1]), ref.dtype)
        ref[0 : PAD - HALO] = zero
        ref[rows - (PAD - HALO) : rows] = zero
    pl.semaphore_wait(barrier, n - 1)

    here = ring_position(patch, n_patch)
    following = ring_patch((here + 1) % n_patch, n_patch)
    before = ring_patch((here + n_patch - 1) % n_patch, n_patch)
    piece = held // (2 * PARTS)

    def ring_copy(way, part, step):
        if way == 0:
            owner = ring_patch((here + n_patch - step) % n_patch, n_patch)
            target = following
        else:
            owner = ring_patch((here + step) % n_patch, n_patch)
            target = before
        block = gath.at[pl.ds(owner * held + (way * PARTS + part) * piece, piece)]
        index = (way * PARTS + part) * (n_patch - 1) + step
        return pltpu.make_async_remote_copy(
            src_ref=block,
            dst_ref=block,
            send_sem=ring_send.at[index],
            recv_sem=ring_recv.at[index],
            device_id={"patch": target, "sub": sub},
            device_id_type=mesh_id,
        )

    def ring_step(step, part):
        for way in (0, 1):
            ring_copy(way, part, step - 1).wait_recv()
            ring_copy(way, part, step).start()

    own_topo.wait()
    for part in range(PARTS):
        for way in (0, 1):
            ring_copy(way, part, 0).start()

    def fault_copy(i):
        return pltpu.make_async_remote_copy(
            src_ref=faults_ref,
            dst_ref=fbuf.at[me],
            send_sem=fault_send.at[i - 1],
            recv_sem=fault_recv.at[i - 1],
            device_id=where((me + i) % n),
            device_id_type=mesh_id,
        )

    def send_fault(i, carry):
        fault_copy(i).start()
        return carry

    lax.fori_loop(1, n, send_fault, 0)

    halos = []
    north, south = where((me + 1) % n), where((me + n - 1) % n)
    for i, (src, dst) in enumerate(pairs):
        rows = src.shape[0]
        up = pltpu.make_async_remote_copy(
            src_ref=src.at[pl.ds(rows - HALO, HALO)],
            dst_ref=dst.at[pl.ds(PAD - HALO, HALO)],
            send_sem=halo_send.at[2 * i],
            recv_sem=halo_recv.at[2 * i],
            device_id=north,
            device_id_type=mesh_id,
        )
        down = pltpu.make_async_remote_copy(
            src_ref=src.at[pl.ds(0, HALO)],
            dst_ref=dst.at[pl.ds(PAD + rows, HALO)],
            send_sem=halo_send.at[2 * i + 1],
            recv_sem=halo_recv.at[2 * i + 1],
            device_id=south,
            device_id_type=mesh_id,
        )
        up.start()
        down.start()
        halos.append((up, down))

    def arrived(indices):
        for i in indices:
            loads[i].wait()
            for copy in halos[i]:
                copy.wait_recv()

    def gather_faults():
        fbuf[me] = faults_ref[...]

        def wait_fault(i, carry):
            fault_copy(i).wait_recv()
            return carry

        lax.fori_loop(1, n, wait_fault, 0)
        for t in range(fpar.shape[1] // LANES):
            fpar[:, t * LANES : (t + 1) * LANES] = jnp.sum(
                fbuf[t * per_tile : (t + 1) * per_tile], axis=0
            )

    def add_uplift(eta, rows_at, cols_at):
        total = eta.shape[0]
        width = eta.shape[1]

        def block(kb, carry):
            at = pl.ds(pl.multiple_of(kb * KB, KB), KB)
            centre_row = fpar[0:1, at]
            centre_col = fpar[1:2, at]
            widths = fpar[2:3, at]
            slips = fpar[3:4, at]
            y = rows_at(lax.broadcasted_iota(jnp.int32, (total, KB), 0))
            along_y = (y.astype(jnp.float32) - centre_row) / widths
            along = jnp.exp(-along_y * along_y) * slips
            x = cols_at(lax.broadcasted_iota(jnp.int32, (width, KB), 0))
            across_x = (x.astype(jnp.float32) - centre_col) / widths
            across = (1.0 + across_x) * jnp.exp(-across_x * across_x)
            eta[...] += lax.dot_general(
                along,
                across,
                (((1,), (1,)), ((), ())),
                precision=lax.Precision.HIGHEST,
                preferred_element_type=jnp.float32,
            )
            return carry

        if fpar.shape[1] == KB:
            block(0, 0)
        else:
            lax.fori_loop(0, fpar.shape[1] // KB, block, 0)

    def coarse_uplift():
        arrived([0])
        add_uplift(etac, lambda i: me * rows_c + i - PAD, lambda i: i)

    def fine_uplift():
        arrived([4])
        add_uplift(
            etaf, lambda i: me * rows_c + i // 2 - PAD // 2, lambda i: first_col + i // 2
        )

    def chunks(body, size, first, last, carry):
        count = (last - first) // size

        def step(i, carry):
            return body(pl.multiple_of(first + (count - 1 - i) * size, 8), carry)

        return lax.fori_loop(0, count, step, carry)

    def no_flux(cols):
        return jnp.zeros((8, cols), jnp.float32)

    lo_c, hi_c = PAD - HALO, PAD + rows_c + HALO
    lo_f, hi_f = PAD - HALO, PAD + rows_f + HALO

    def coarse_step():
        arrived([1, 2, 3])

        def body(b, flux_above):
            at = pl.ds(b, COARSE_CH)
            col = lax.broadcasted_iota(jnp.int32, (COARSE_CH, cols_c), 1)
            row = lax.broadcasted_iota(jnp.int32, (COARSE_CH, cols_c), 0) + (
                me * rows_c + b - PAD
            )
            eta, h = etac[at], hc[at]
            u = jnp.where(col > 0, uc[at] - courant * (eta - west(eta)), 0.0)
            flux_x = 0.5 * (h + west(h)) * u
            v = vc[at] - courant * (eta - south_of(etac, b, eta))
            v = jnp.where((row >= 1) & (row < n * rows_c), v, 0.0)
            flux_y = 0.5 * (h + south_of(hc, b, h)) * v
            uc[at] = u
            vc[at] = v
            spread = east(flux_x) - flux_x + north_of(flux_y, flux_above) - flux_y
            etac1[at] = eta - courant * spread
            return flux_y[:8]

        chunks(body, COARSE_CH, lo_c, hi_c, no_flux(cols_c))
        write(etac1, eta_c_out)
        write(uc, u_c_out)
        write(vc, v_c_out)

    outs = []

    def write(src, dst, first=0, last=None):
        rows = (dst.shape[0] if last is None else last) - first
        copy = pltpu.make_async_copy(
            src.at[pl.ds(PAD + first, rows)],
            dst.at[pl.ds(first, rows)],
            out_sem.at[len(outs)],
        )
        copy.start()
        outs.append(copy)

    def ghosts():
        rows = ghost1.shape[0]
        coarse = lax.broadcasted_iota(jnp.int32, (rows, etac.shape[0]), 1)
        fine = lax.broadcasted_iota(jnp.int32, (rows, etac.shape[0]), 0)
        spread = (coarse == fine // 2 + PAD // 2).astype(jnp.float32)
        old = etac[:, first_col - LANES : first_col]
        new = etac1[:, first_col - LANES : first_col]
        for ref, value in ((ghost1, old + 0.5 * (new - old)), (ghost2, new)):
            ref[...] = west(
                jnp.dot(
                    spread,
                    value,
                    precision=lax.Precision.HIGHEST,
                    preferred_element_type=jnp.float32,
                )
            )

    def eta_west(eta, ghost, col):
        return jnp.where(
            col == 0, jnp.concatenate([ghost] * (cols_f // LANES), 1), west(eta)
        )

    def fine_masks():
        arrived([5, 6, 7])
        wet[lo_f:PAD] = wet[lo_f:PAD] * (me + n - 1) // n
        wet[PAD + rows_f : hi_f] = wet[PAD + rows_f : hi_f] * (
            (2 * n - 2 - me) // n
        )
        wetf[...] = wet[...].astype(jnp.float32)

    def fine_first():
        def body(b, carry):
            at = pl.ds(b, FINE_CH)
            col = lax.broadcasted_iota(jnp.int32, (FINE_CH, cols_f), 1)
            m = wetf[at]
            mw = m * jnp.where(col == 0, 1.0, west(m))
            mm = m * south_of(wetf, b, m)
            eta = etaf[at]
            mwf[at] = mw
            mmf[at] = mm
            uf[at] = (uf[at] - courant * (eta - eta_west(eta, ghost1[at], col))) * mw
            vf[at] = (vf[at] - courant * (eta - south_of(etaf, b, eta))) * mm
            return carry

        chunks(body, FINE_CH, lo_f, hi_f, 0)

    work = [
        gather_faults,
        coarse_uplift,
        coarse_step,
        ghosts,
        fine_uplift,
        fine_masks,
        fine_first,
    ]
    shown = min(n_patch - 1, 7)
    for step in range(1, shown):
        for part in range(PARTS):
            if work:
                work.pop(0)()
            ring_step(step, part)
    for piece_of_work in work:
        piece_of_work()
    if shown < n_patch - 1:

        def later(step, carry):
            for part in range(PARTS):
                ring_step(step, part)
            return carry

        lax.fori_loop(shown, n_patch - 1, later, 0)
    for part in range(PARTS):
        for way in (0, 1):
            ring_copy(way, part, n_patch - 2).wait_recv()

    for copy in lists[:2]:
        copy.wait()
    count = rows_f // FP

    def take(first, dst, row):
        tiles = [
            gath[owners[first + j] * held + blocks[first + j]] for j in range(4)
        ]
        for t in range(cols_f // LANES):
            dst[pl.ds(row, 8), t * LANES : (t + 1) * LANES] = jnp.concatenate(
                [b[t * FP : (t + 1) * FP] for b in tiles], 0
            )

    mate = patch * n_sub + (n_sub - 1 - sub)
    take((mate * count + n * count - 4) % (n * count), rim, 0)
    take((mate * count + count) % (n * count), rim, 8)
    rims = []
    for i, to in enumerate((PAD - HALO, PAD + rows_f)):
        copy = pltpu.make_async_remote_copy(
            src_ref=rim.at[pl.ds(i * HALO, HALO)],
            dst_ref=hf.at[pl.ds(to, HALO)],
            send_sem=rim_send.at[i],
            recv_sem=rim_recv.at[i],
            device_id={"patch": patch, "sub": n_sub - 1 - sub},
            device_id_type=mesh_id,
        )
        copy.start()
        rims.append(copy)

    def take_own(i, carry):
        take(me * count + i * 4, hf, pl.multiple_of(PAD + i * 8, 8))
        return carry

    lax.fori_loop(0, rows_f // 8, take_own, 0, unroll=4)
    for copy in rims:
        copy.wait()

    def fine_flux(b, flux_above):
        at = pl.ds(b, FINE_CH)
        col = lax.broadcasted_iota(jnp.int32, (FINE_CH, cols_f), 1)
        h = hf[at]
        hw = jnp.where(col == 0, h, 0.5 * (h + west(h)))
        hs = 0.5 * (h + south_of(hf, b, h))
        flux_x = hw * uf[at]
        flux_y = hs * vf[at]
        hwf[at] = hw
        hsf[at] = hs
        flux_east = jnp.where(col == cols_f - 1, 0.0, east(flux_x))
        spread = flux_east - flux_x + north_of(flux_y, flux_above) - flux_y
        etaf[at] = etaf[at] - courant * spread
        return flux_y[:8]

    chunks(fine_flux, FINE_CH, lo_f, hi_f, no_flux(cols_f))

    def fine_second(b, flux_above):
        at = pl.ds(b, FINE_CH)
        col = lax.broadcasted_iota(jnp.int32, (FINE_CH, cols_f), 1)
        eta = etaf[at]
        u = (uf[at] - courant * (eta - eta_west(eta, ghost2[at], col))) * mwf[at]
        v = (vf[at] - courant * (eta - south_of(etaf, b, eta))) * mmf[at]
        flux_x = hwf[at] * u
        flux_y = hsf[at] * v
        uf[at] = u
        vf[at] = v
        flux_east = jnp.where(col == cols_f - 1, 0.0, east(flux_x))
        spread = flux_east - flux_x + north_of(flux_y, flux_above) - flux_y
        etap[at] = eta - courant * spread
        return flux_y[:8]

    carry = no_flux(cols_f)
    segment = (hi_f - lo_f) // SEGMENTS
    for k in range(SEGMENTS - 1, -1, -1):
        first = lo_f + k * segment
        carry = chunks(fine_second, FINE_CH, first, first + segment, carry)
        own = (max(first - PAD, 0), min(first + segment - PAD, rows_f))
        for src, dst in ((uf, u_f_out), (vf, v_f_out), (etap, eta_f_out)):
            write(src, dst, *own)

    def sent(i, carry):
        fault_copy(i).wait_send()
        return carry

    lax.fori_loop(1, n, sent, 0)
    for up, down in halos:
        up.wait_send()
        down.wait_send()

    def passed(step, carry):
        for part in range(PARTS):
            for way in (0, 1):
                ring_copy(way, part, step).wait_send()
        return carry

    lax.fori_loop(0, n_patch - 1, passed, 0)
    for copy in outs:
        copy.wait()


def hand_over(*refs):
    results, outputs, staged = refs[:6], refs[6:12], refs[12:18]
    read_sem, write_sem = refs[18:]
    reads, writes = [], []
    for i in (2, 1, 0, 5, 4, 3):
        rows = results[i].shape[0] // SLABS
        for j in range(SLABS):
            at = pl.ds(j * rows, rows)
            k = i * SLABS + j
            reads.append(
                pltpu.make_async_copy(
                    results[i].at[at], staged[i].at[at], read_sem.at[k]
                )
            )
            writes.append(
                pltpu.make_async_copy(
                    staged[i].at[at], outputs[i].at[at], write_sem.at[k]
                )
            )
    for copy in reads:
        copy.start()
    for read, write in zip(reads, writes):
        read.wait()
        write.start()
    for copy in writes:
        copy.wait()


def on_device(
    eta_c,
    u_c,
    v_c,
    depth_c,
    eta_f,
    u_f,
    v_f,
    wet_f,
    topography,
    owner_list,
    block_list,
    fault_row,
    fault_col,
    fault_width,
    fault_slip,
):
    rows_c, cols_c = eta_c.shape
    rows_f, cols_f = eta_f.shape
    n_patch = lax.axis_size("patch")
    n_sub = lax.axis_size("sub")
    n = n_patch * n_sub
    held = topography.shape[0]
    mine = fault_row.shape[0]
    tiles = (
        topography.reshape(held, FP, cols_f // LANES, LANES)
        .transpose(0, 2, 1, 3)
        .reshape(held, FP * cols_f // LANES, LANES)
    )
    f32 = jnp.float32
    coarse = pltpu.VMEM((rows_c + 2 * PAD, cols_c), f32)
    fine = pltpu.VMEM((rows_f + 2 * PAD, cols_f), f32)
    dma = pltpu.SemaphoreType.DMA
    any_spec = pl.BlockSpec(memory_space=pl.ANY)
    results = pl.pallas_call(
        functools.partial(kernel, n_patch, n_sub),
        out_shape=[jax.ShapeDtypeStruct((rows_c, cols_c), f32)] * 3
        + [jax.ShapeDtypeStruct((rows_f, cols_f), f32)] * 3,
        in_specs=[any_spec] * 15,
        out_specs=[any_spec] * 6,
        scratch_shapes=[
            pltpu.SMEM(block_list.shape, jnp.int32),
            pltpu.SMEM(block_list.shape, jnp.int32),
            pltpu.SMEM((4, mine), f32),
            pltpu.VMEM((8, LANES), f32),
            pltpu.VMEM((n_patch * held,) + tiles.shape[1:], f32),
            pltpu.VMEM((n, 8, LANES), f32),
            pltpu.VMEM((8, n * mine), f32),
        ]
        + [coarse] * 5
        + [fine] * 4
        + [pltpu.VMEM((rows_f + 2 * PAD, cols_f), jnp.int32)]
        + [fine] * 6
        + [pltpu.VMEM((2 * HALO, cols_f), f32)]
        + [pltpu.VMEM((rows_f + 2 * PAD, LANES), f32)] * 2
        + [
            dma((15,)),
            dma((3 + 3 * SEGMENTS,)),
            dma((2 * PARTS * (n_patch - 1),)),
            dma((2 * PARTS * (n_patch - 1),)),
            dma((n - 1,)),
            dma((n - 1,)),
            dma((16,)),
            dma((16,)),
            dma((2,)),
            dma((2,)),
        ],
        compiler_params=pltpu.CompilerParams(
            collective_id=0, has_side_effects=True, vmem_limit_bytes=60 * 2**20
        ),
    )(
        owner_list.reshape(-1),
        block_list,
        fault_row,
        fault_col,
        fault_width,
        fault_slip,
        eta_c,
        u_c,
        v_c,
        depth_c,
        eta_f,
        u_f,
        v_f,
        wet_f,
        tiles,
    )
    return pl.pallas_call(
        hand_over,
        out_shape=[jax.ShapeDtypeStruct(r.shape, r.dtype) for r in results],
        in_specs=[any_spec] * 6,
        out_specs=[any_spec] * 6,
        scratch_shapes=[pltpu.VMEM(r.shape, r.dtype) for r in results]
        + [dma((6 * SLABS,))] * 2,
        compiler_params=pltpu.CompilerParams(vmem_limit_bytes=60 * 2**20),
    )(*results)


def solution(mesh):
    rows = P(("runs", "patch", "sub"), None)
    line = P(("runs", "patch", "sub"))
    return jax.shard_map(
        on_device,
        mesh=mesh,
        in_specs=(rows,) * 8
        + (P(("runs", "patch", "sub"), None, None), P("runs", None), P("runs"))
        + (line,) * 4,
        out_specs=(rows,) * 6,
        check_vma=False,
    )
```

```python
import functools

import jax
import jax.numpy as jnp
from jax import lax
from jax.experimental import pallas as pl
from jax.experimental.pallas import tpu as pltpu
from jax.sharding import PartitionSpec as P

FP = 2
LANES = 128
PAD = 16
HALO = 8
COARSE_CH = 16
FINE_CH = 80
SEGMENTS = 5
KB = 256
PARTS = 3
SLABS = 2

courant = 0.35


def west(x):
    return pltpu.roll(x, 1, 1)


def east(x):
    return pltpu.roll(x, x.shape[1] - 1, 1)


def south_of(ref, b, here):
    edge = ref[pl.ds(pl.multiple_of(b - 8, 8), 8)]
    return pltpu.roll(jnp.concatenate([edge, here], 0), 1, 0)[8:]


def north_of(here, above):
    rows = here.shape[0]
    return pltpu.roll(jnp.concatenate([here, above], 0), rows + 7, 0)[:rows]


def ring_position(p, n):
    odd = p % 2
    return (1 - odd) * (p // 2) + odd * (n - 1 - p // 2)


def ring_patch(k, n):
    back = k // (n // 2)
    return (1 - back) * (2 * k) + back * (2 * (n - 1 - k) + 1)


def kernel(
    n_patch,
    n_sub,
    owner_in,
    block_in,
    row_in,
    col_in,
    width_in,
    slip_in,
    eta_c_in,
    u_c_in,
    v_c_in,
    depth_c_in,
    eta_f_in,
    u_f_in,
    v_f_in,
    wet_f_in,
    topo_in,
    eta_c_out,
    u_c_out,
    v_c_out,
    eta_f_out,
    u_f_out,
    v_f_out,
    owners,
    blocks,
    params,
    faults_ref,
    gath,
    fbuf,
    fpar,
    etac,
    uc,
    vc,
    hc,
    etac1,
    etaf,
    uf,
    vf,
    wetf,
    wet,
    mwf,
    mmf,
    hf,
    hwf,
    hsf,
    etap,
    rim,
    ghost1,
    ghost2,
    local_sem,
    out_sem,
    ring_send,
    ring_recv,
    fault_send,
    fault_recv,
    halo_send,
    halo_recv,
    rim_send,
    rim_recv,
):
    mesh_id = pl.DeviceIdType.MESH
    patch = lax.axis_index("patch")
    sub = lax.axis_index("sub")
    n = n_patch * n_sub
    me = patch * n_sub + sub
    rows_c, cols_c = eta_c_in.shape
    rows_f, cols_f = eta_f_in.shape
    held = topo_in.shape[0]
    first_col = cols_c - cols_f // 2

    def where(flat):
        return {"patch": flat // n_sub, "sub": flat % n_sub}

    own_topo = pltpu.make_async_copy(
        topo_in, gath.at[pl.ds(patch * held, held)], local_sem.at[8]
    )
    own_topo.start()
    pairs = [
        (eta_c_in, etac),
        (u_c_in, uc),
        (v_c_in, vc),
        (depth_c_in, hc),
        (eta_f_in, etaf),
        (u_f_in, uf),
        (v_f_in, vf),
        (wet_f_in, wet),
    ]
    loads = []
    for i, (src, dst) in enumerate(pairs):
        copy = pltpu.make_async_copy(
            src, dst.at[pl.ds(PAD, src.shape[0])], local_sem.at[i]
        )
        copy.start()
        loads.append(copy)

    lists = []
    for i, (src, dst) in enumerate(
        (
            (owner_in, owners),
            (block_in, blocks),
            (row_in, params.at[0]),
            (col_in, params.at[1]),
            (width_in, params.at[2]),
            (slip_in, params.at[3]),
        )
    ):
        copy = pltpu.make_async_copy(src, dst, local_sem.at[9 + i])
        copy.start()
        lists.append(copy)

    barrier = pltpu.get_barrier_semaphore()

    def greet(i, carry):
        pl.semaphore_signal(
            barrier, inc=1, device_id=where((me + i) % n), device_id_type=mesh_id
        )
        return carry

    lax.fori_loop(1, n, greet, 0)
    per_tile = LANES * n // fpar.shape[1]
    for copy in lists[2:]:
        copy.wait()
    line = lax.broadcasted_iota(jnp.int32, (8, LANES), 0)
    lane = lax.broadcasted_iota(jnp.int32, (8, LANES), 1)
    lane = lane - (me % per_tile) * (LANES // per_tile)
    tile = jnp.zeros((8, LANES), jnp.float32)
    for i in range(4):
        for j in range(LANES // per_tile):
            tile = jnp.where((line == i) & (lane == j), params[i, j], tile)
    faults_ref[...] = tile
    for ref in (etac, hc, etac1, etaf, hf, wet):
        rows = ref.shape[0]
        zero = jnp.zeros((PAD - HALO, ref.shape[1]), ref.dtype)
        ref[0 : PAD - HALO] = zero
        ref[rows - (PAD - HALO) : rows] = zero
    pl.semaphore_wait(barrier, n - 1)

    here = ring_position(patch, n_patch)
    following = ring_patch((here + 1) % n_patch, n_patch)
    before = ring_patch((here + n_patch - 1) % n_patch, n_patch)
    piece = held // (2 * PARTS)

    def ring_copy(way, part, step):
        if way == 0:
            owner = ring_patch((here + n_patch - step) % n_patch, n_patch)
            target = following
        else:
            owner = ring_patch((here + step) % n_patch, n_patch)
            target = before
        block = gath.at[pl.ds(owner * held + (way * PARTS + part) * piece, piece)]
        source = block
        if isinstance(step, int) and step == 0:
            source = topo_in.at[pl.ds((way * PARTS + part) * piece, piece)]
        index = (way * PARTS + part) * (n_patch - 1) + step
        return pltpu.make_async_remote_copy(
            src_ref=source,
            dst_ref=block,
            send_sem=ring_send.at[index],
            recv_sem=ring_recv.at[index],
            device_id={"patch": target, "sub": sub},
            device_id_type=mesh_id,
        )

    def ring_step(step, part):
        for way in (0, 1):
            ring_copy(way, part, step - 1).wait_recv()
            ring_copy(way, part, step).start()

    for part in range(PARTS):
        for way in (0, 1):
            ring_copy(way, part, 0).start()

    def fault_copy(i):
        return pltpu.make_async_remote_copy(
            src_ref=faults_ref,
            dst_ref=fbuf.at[me],
            send_sem=fault_send.at[i - 1],
            recv_sem=fault_recv.at[i - 1],
            device_id=where((me + i) % n),
            device_id_type=mesh_id,
        )

    def send_fault(i, carry):
        fault_copy(i).start()
        return carry

    lax.fori_loop(1, n, send_fault, 0)

    halos = []
    north, south = where((me + 1) % n), where((me + n - 1) % n)
    for i, (src, dst) in enumerate(pairs):
        rows = src.shape[0]
        up = pltpu.make_async_remote_copy(
            src_ref=src.at[pl.ds(rows - HALO, HALO)],
            dst_ref=dst.at[pl.ds(PAD - HALO, HALO)],
            send_sem=halo_send.at[2 * i],
            recv_sem=halo_recv.at[2 * i],
            device_id=north,
            device_id_type=mesh_id,
        )
        down = pltpu.make_async_remote_copy(
            src_ref=src.at[pl.ds(0, HALO)],
            dst_ref=dst.at[pl.ds(PAD + rows, HALO)],
            send_sem=halo_send.at[2 * i + 1],
            recv_sem=halo_recv.at[2 * i + 1],
            device_id=south,
            device_id_type=mesh_id,
        )
        up.start()
        down.start()
        halos.append((up, down))

    def arrived(indices):
        for i in indices:
            loads[i].wait()
            for copy in halos[i]:
                copy.wait_recv()

    def gather_faults():
        fbuf[me] = faults_ref[...]

        def wait_fault(i, carry):
            fault_copy(i).wait_recv()
            return carry

        lax.fori_loop(1, n, wait_fault, 0)
        for t in range(fpar.shape[1] // LANES):
            fpar[:, t * LANES : (t + 1) * LANES] = jnp.sum(
                fbuf[t * per_tile : (t + 1) * per_tile], axis=0
            )

    def add_uplift(eta, rows_at, cols_at):
        total = eta.shape[0]
        width = eta.shape[1]

        def block(kb, carry):
            at = pl.ds(pl.multiple_of(kb * KB, KB), KB)
            centre_row = fpar[0:1, at]
            centre_col = fpar[1:2, at]
            widths = fpar[2:3, at]
            slips = fpar[3:4, at]
            y = rows_at(lax.broadcasted_iota(jnp.int32, (total, KB), 0))
            along_y = (y.astype(jnp.float32) - centre_row) / widths
            along = jnp.exp(-along_y * along_y) * slips
            x = cols_at(lax.broadcasted_iota(jnp.int32, (width, KB), 0))
            across_x = (x.astype(jnp.float32) - centre_col) / widths
            across = (1.0 + across_x) * jnp.exp(-across_x * across_x)
            eta[...] += lax.dot_general(
                along,
                across,
                (((1,), (1,)), ((), ())),
                precision=lax.Precision.HIGHEST,
                preferred_element_type=jnp.float32,
            )
            return carry

        if fpar.shape[1] == KB:
            block(0, 0)
        else:
            lax.fori_loop(0, fpar.shape[1] // KB, block, 0)

    def coarse_uplift():
        arrived([0])
        add_uplift(etac, lambda i: me * rows_c + i - PAD, lambda i: i)

    def fine_uplift():
        arrived([4])
        add_uplift(
            etaf, lambda i: me * rows_c + i // 2 - PAD // 2, lambda i: first_col + i // 2
        )

    def chunks(body, size, first, last, carry):
        count = (last - first) // size

        def step(i, carry):
            return body(pl.multiple_of(first + (count - 1 - i) * size, 8), carry)

        return lax.fori_loop(0, count, step, carry)

    def no_flux(cols):
        return jnp.zeros((8, cols), jnp.float32)

    lo_c, hi_c = PAD - HALO, PAD + rows_c + HALO
    lo_f, hi_f = PAD - HALO, PAD + rows_f + HALO

    def coarse_step():
        arrived([1, 2, 3])

        def body(b, flux_above):
            at = pl.ds(b, COARSE_CH)
            col = lax.broadcasted_iota(jnp.int32, (COARSE_CH, cols_c), 1)
            row = lax.broadcasted_iota(jnp.int32, (COARSE_CH, cols_c), 0) + (
                me * rows_c + b - PAD
            )
            eta, h = etac[at], hc[at]
            u = jnp.where(col > 0, uc[at] - courant * (eta - west(eta)), 0.0)
            flux_x = 0.5 * (h + west(h)) * u
            v = vc[at] - courant * (eta - south_of(etac, b, eta))
            v = jnp.where((row >= 1) & (row < n * rows_c), v, 0.0)
            flux_y = 0.5 * (h + south_of(hc, b, h)) * v
            uc[at] = u
            vc[at] = v
            spread = east(flux_x) - flux_x + north_of(flux_y, flux_above) - flux_y
            etac1[at] = eta - courant * spread
            return flux_y[:8]

        chunks(body, COARSE_CH, lo_c, hi_c, no_flux(cols_c))
        write(etac1, eta_c_out)
        write(uc, u_c_out)
        write(vc, v_c_out)

    outs = []

    def write(src, dst, first=0, last=None):
        rows = (dst.shape[0] if last is None else last) - first
        copy = pltpu.make_async_copy(
            src.at[pl.ds(PAD + first, rows)],
            dst.at[pl.ds(first, rows)],
            out_sem.at[len(outs)],
        )
        copy.start()
        outs.append(copy)

    def ghosts():
        rows = ghost1.shape[0]
        coarse = lax.broadcasted_iota(jnp.int32, (rows, etac.shape[0]), 1)
        fine = lax.broadcasted_iota(jnp.int32, (rows, etac.shape[0]), 0)
        spread = (coarse == fine // 2 + PAD // 2).astype(jnp.float32)
        old = etac[:, first_col - LANES : first_col]
        new = etac1[:, first_col - LANES : first_col]
        for ref, value in ((ghost1, old + 0.5 * (new - old)), (ghost2, new)):
            ref[...] = west(
                jnp.dot(
                    spread,
                    value,
                    precision=lax.Precision.HIGHEST,
                    preferred_element_type=jnp.float32,
                )
            )

    def eta_west(eta, ghost, col):
        return jnp.where(
            col == 0, jnp.concatenate([ghost] * (cols_f // LANES), 1), west(eta)
        )

    def fine_masks():
        arrived([5, 6, 7])
        wet[lo_f:PAD] = wet[lo_f:PAD] * (me + n - 1) // n
        wet[PAD + rows_f : hi_f] = wet[PAD + rows_f : hi_f] * (
            (2 * n - 2 - me) // n
        )
        wetf[...] = wet[...].astype(jnp.float32)

    def fine_first():
        def body(b, carry):
            at = pl.ds(b, FINE_CH)
            col = lax.broadcasted_iota(jnp.int32, (FINE_CH, cols_f), 1)
            m = wetf[at]
            mw = m * jnp.where(col == 0, 1.0, west(m))
            mm = m * south_of(wetf, b, m)
            eta = etaf[at]
            mwf[at] = mw
            mmf[at] = mm
            uf[at] = (uf[at] - courant * (eta - eta_west(eta, ghost1[at], col))) * mw
            vf[at] = (vf[at] - courant * (eta - south_of(etaf, b, eta))) * mm
            return carry

        chunks(body, FINE_CH, lo_f, hi_f, 0)

    work = [
        gather_faults,
        coarse_uplift,
        coarse_step,
        ghosts,
        fine_uplift,
        fine_masks,
        fine_first,
    ]
    shown = min(n_patch - 1, 7)
    for step in range(1, shown):
        for part in range(PARTS):
            if work and part < 2:
                work.pop(0)()
            ring_step(step, part)
    for piece_of_work in work:
        piece_of_work()
    if shown < n_patch - 1:

        def later(step, carry):
            for part in range(PARTS):
                ring_step(step, part)
            return carry

        lax.fori_loop(shown, n_patch - 1, later, 0)
    for part in range(PARTS):
        for way in (0, 1):
            ring_copy(way, part, n_patch - 2).wait_recv()

    own_topo.wait()

    for copy in lists[:2]:
        copy.wait()
    count = rows_f // FP

    def take(first, dst, row):
        tiles = [
            gath[owners[first + j] * held + blocks[first + j]] for j in range(4)
        ]
        for t in range(cols_f // LANES):
            dst[pl.ds(row, 8), t * LANES : (t + 1) * LANES] = jnp.concatenate(
                [b[t * FP : (t + 1) * FP] for b in tiles], 0
            )

    mate = patch * n_sub + (n_sub - 1 - sub)
    take((mate * count + n * count - 4) % (n * count), rim, 0)
    take((mate * count + count) % (n * count), rim, 8)
    rims = []
    for i, to in enumerate((PAD - HALO, PAD + rows_f)):
        copy = pltpu.make_async_remote_copy(
            src_ref=rim.at[pl.ds(i * HALO, HALO)],
            dst_ref=hf.at[pl.ds(to, HALO)],
            send_sem=rim_send.at[i],
            recv_sem=rim_recv.at[i],
            device_id={"patch": patch, "sub": n_sub - 1 - sub},
            device_id_type=mesh_id,
        )
        copy.start()
        rims.append(copy)

    def take_own(i, carry):
        take(me * count + i * 4, hf, pl.multiple_of(PAD + i * 8, 8))
        return carry

    lax.fori_loop(0, rows_f // 8, take_own, 0, unroll=4)
    for copy in rims:
        copy.wait()

    def fine_flux(b, flux_above):
        at = pl.ds(b, 2 * FINE_CH + 40)
        col = lax.broadcasted_iota(jnp.int32, (2 * FINE_CH + 40, cols_f), 1)
        h = hf[at]
        hw = jnp.where(col == 0, h, 0.5 * (h + west(h)))
        hs = 0.5 * (h + south_of(hf, b, h))
        flux_x = hw * uf[at]
        flux_y = hs * vf[at]
        hwf[at] = hw
        hsf[at] = hs
        flux_east = jnp.where(col == cols_f - 1, 0.0, east(flux_x))
        spread = flux_east - flux_x + north_of(flux_y, flux_above) - flux_y
        etaf[at] = etaf[at] - courant * spread
        return flux_y[:8]

    chunks(fine_flux, 2 * FINE_CH + 40, lo_f, hi_f, no_flux(cols_f))

    def fine_second(b, flux_above):
        at = pl.ds(b, FINE_CH)
        col = lax.broadcasted_iota(jnp.int32, (FINE_CH, cols_f), 1)
        eta = etaf[at]
        u = (uf[at] - courant * (eta - eta_west(eta, ghost2[at], col))) * mwf[at]
        v = (vf[at] - courant * (eta - south_of(etaf, b, eta))) * mmf[at]
        flux_x = hwf[at] * u
        flux_y = hsf[at] * v
        uf[at] = u
        vf[at] = v
        flux_east = jnp.where(col == cols_f - 1, 0.0, east(flux_x))
        spread = flux_east - flux_x + north_of(flux_y, flux_above) - flux_y
        etap[at] = eta - courant * spread
        return flux_y[:8]

    carry = no_flux(cols_f)
    segment = (hi_f - lo_f) // SEGMENTS
    for k in range(SEGMENTS - 1, -1, -1):
        first = lo_f + k * segment
        carry = chunks(fine_second, FINE_CH, first, first + segment, carry)
        own = (max(first - PAD, 0), min(first + segment - PAD, rows_f))
        for src, dst in ((uf, u_f_out), (vf, v_f_out), (etap, eta_f_out)):
            write(src, dst, *own)

    def sent(i, carry):
        fault_copy(i).wait_send()
        return carry

    lax.fori_loop(1, n, sent, 0)
    for up, down in halos:
        up.wait_send()
        down.wait_send()

    def passed(step, carry):
        for part in range(PARTS):
            for way in (0, 1):
                ring_copy(way, part, step).wait_send()
        return carry

    lax.fori_loop(0, n_patch - 1, passed, 0)
    for copy in outs:
        copy.wait()


def hand_over(*refs):
    results, outputs, staged = refs[:6], refs[6:12], refs[12:18]
    read_sem, write_sem = refs[18:]
    reads, writes = [], []
    for i in (2, 1, 0, 5, 4, 3):
        rows = results[i].shape[0] // SLABS
        for j in range(SLABS):
            at = pl.ds(j * rows, rows)
            k = i * SLABS + j
            reads.append(
                pltpu.make_async_copy(
                    results[i].at[at], staged[i].at[at], read_sem.at[k]
                )
            )
            writes.append(
                pltpu.make_async_copy(
                    staged[i].at[at], outputs[i].at[at], write_sem.at[k]
                )
            )
    for copy in reads:
        copy.start()
    for read, write in zip(reads, writes):
        read.wait()
        write.start()
    for copy in writes:
        copy.wait()


def on_device(
    eta_c,
    u_c,
    v_c,
    depth_c,
    eta_f,
    u_f,
    v_f,
    wet_f,
    topography,
    owner_list,
    block_list,
    fault_row,
    fault_col,
    fault_width,
    fault_slip,
):
    rows_c, cols_c = eta_c.shape
    rows_f, cols_f = eta_f.shape
    n_patch = lax.axis_size("patch")
    n_sub = lax.axis_size("sub")
    n = n_patch * n_sub
    held = topography.shape[0]
    mine = fault_row.shape[0]
    tiles = (
        topography.reshape(held, FP, cols_f // LANES, LANES)
        .transpose(0, 2, 1, 3)
        .reshape(held, FP * cols_f // LANES, LANES)
    )
    f32 = jnp.float32
    coarse = pltpu.VMEM((rows_c + 2 * PAD, cols_c), f32)
    fine = pltpu.VMEM((rows_f + 2 * PAD, cols_f), f32)
    dma = pltpu.SemaphoreType.DMA
    any_spec = pl.BlockSpec(memory_space=pl.ANY)
    results = pl.pallas_call(
        functools.partial(kernel, n_patch, n_sub),
        out_shape=[jax.ShapeDtypeStruct((rows_c, cols_c), f32)] * 3
        + [jax.ShapeDtypeStruct((rows_f, cols_f), f32)] * 3,
        in_specs=[any_spec] * 15,
        out_specs=[any_spec] * 6,
        scratch_shapes=[
            pltpu.SMEM(block_list.shape, jnp.int32),
            pltpu.SMEM(block_list.shape, jnp.int32),
            pltpu.SMEM((4, mine), f32),
            pltpu.VMEM((8, LANES), f32),
            pltpu.VMEM((n_patch * held,) + tiles.shape[1:], f32),
            pltpu.VMEM((n, 8, LANES), f32),
            pltpu.VMEM((8, n * mine), f32),
        ]
        + [coarse] * 5
        + [fine] * 4
        + [pltpu.VMEM((rows_f + 2 * PAD, cols_f), jnp.int32)]
        + [fine] * 6
        + [pltpu.VMEM((2 * HALO, cols_f), f32)]
        + [pltpu.VMEM((rows_f + 2 * PAD, LANES), f32)] * 2
        + [
            dma((15,)),
            dma((3 + 3 * SEGMENTS,)),
            dma((2 * PARTS * (n_patch - 1),)),
            dma((2 * PARTS * (n_patch - 1),)),
            dma((n - 1,)),
            dma((n - 1,)),
            dma((16,)),
            dma((16,)),
            dma((2,)),
            dma((2,)),
        ],
        compiler_params=pltpu.CompilerParams(
            collective_id=0, has_side_effects=True, vmem_limit_bytes=60 * 2**20
        ),
    )(
        owner_list.reshape(-1),
        block_list,
        fault_row,
        fault_col,
        fault_width,
        fault_slip,
        eta_c,
        u_c,
        v_c,
        depth_c,
        eta_f,
        u_f,
        v_f,
        wet_f,
        tiles,
    )
    return pl.pallas_call(
        hand_over,
        out_shape=[jax.ShapeDtypeStruct(r.shape, r.dtype) for r in results],
        in_specs=[any_spec] * 6,
        out_specs=[any_spec] * 6,
        scratch_shapes=[pltpu.VMEM(r.shape, r.dtype) for r in results]
        + [dma((6 * SLABS,))] * 2,
        compiler_params=pltpu.CompilerParams(vmem_limit_bytes=60 * 2**20),
    )(*results)


def solution(mesh):
    rows = P(("runs", "patch", "sub"), None)
    line = P(("runs", "patch", "sub"))
    return jax.shard_map(
        on_device,
        mesh=mesh,
        in_specs=(rows,) * 8
        + (P(("runs", "patch", "sub"), None, None), P("runs", None), P("runs"))
        + (line,) * 4,
        out_specs=(rows,) * 6,
        check_vma=False,
    )
```
